32 devices in a mesh: grp: 2 (over x), lat: 8 (over z, y), row: 2 (over core).
Axes of the slice: x: 2, y: 2, z: 4, core: 2. Of those that a mesh axis runs over, the one named last changes fastest.
Arguments:
- activations: bfloat16 [2560, 4096], P(('grp', 'row')), parts along dimension 0, may hold values from -6 to 6
- enc_weight: float32 [8192, 8192], P(('grp', 'row'), 'lat'), parts along dimension 0, may hold values from -0.09375 to 0.09375
- dec_weight: float32 [16384, 4096], P(('grp', 'lat'), 'row'), parts along dimension 0, may hold values from -0.0625 to 0.0625
- enc_bias: float32 [16384], P(('grp', 'lat')), parts along dimension 0, may hold values from -3 to 3
- dec_bias: float32 [8192], P('grp'), parts along dimension 0, may hold values from -3 to 3
- enc_first: bfloat16 [8192, 8192], P(('grp', 'row'), 'lat'), parts along dimension 0, may hold values from -0.125 to 0.125
- enc_second: bfloat16 [8192, 8192], P(('grp', 'row'), 'lat'), parts along dimension 0, may hold values from 1.9520521e-06 to 0.00019454956
- dec_first: bfloat16 [16384, 4096], P(('grp', 'lat'), 'row'), parts along dimension 0, may hold values from -0.125 to 0.125
- dec_second: bfloat16 [16384, 4096], P(('grp', 'lat'), 'row'), parts along dimension 0, may hold values from 1.9520521e-06 to 0.00019454956
Outputs:
- enc_step: bfloat16 [8192, 8192], P(('grp', 'row'), 'lat'), parts along dimension 0
- dec_step: bfloat16 [16384, 4096], P(('grp', 'lat'), 'row'), parts along dimension 0
The draws below stay inside these ranges and needn't reach their ends.
There are 2 independent parts, one for each index of `grp`. The reference program is written for one: setup_inputs(seed, part) draws one part's arguments, and reference() takes and returns one part's arrays. A program takes and returns all parts, laid end to end along the dimension named above; each array names one. Nothing has to cross between parts.
All inputs are finite; a program needn't handle non-finite values.
Results may differ from the reference program's by a relative error of at most 0.012.
The reference program's roundings to bfloat16 on the way (of `centered`, `latent_codes`, `residual_grad` and `pre_grad`) count: a program that leaves them out, or rounds other values in their place, can miss the bound.
Values may be sent and summed in bfloat16 or wider, within the bound.
A program may use at most 192 MiB of HBM per device.

```python
import math
import jax
import jax.numpy as jnp

D = 4096
LAT = 8192
ROWS = 1280


def level_of(own_key, extent, cuts, least, largest):
    gain = 1.0
    for dim, parts in cuts:
        steps = jax.random.uniform(jax.random.fold_in(jax.random.fold_in(own_key, 6), dim), (parts,), jnp.float32, least / len(cuts), largest / len(cuts))
        gain = gain * jnp.repeat(jnp.exp(steps), extent[dim] // parts).reshape((-1,) + (1,) * (len(extent) - 1 - dim))
    return gain


def noise(rng, dims, spread, bound, split=(), kind=jnp.bfloat16):
    factor_of = level_of(rng, dims, split, -0.22, 0.18) if split else 1.0
    array = jax.random.normal(rng, dims, jnp.float32) * spread * factor_of
    return jnp.minimum(jnp.maximum(array, -bound), bound).astype(kind)


def setup_inputs(seed: int = 0, part: int = 0) -> dict:
    seeds = jax.random.split(jax.random.key(seed), 10)
    part_keys = jax.random.split(jax.random.fold_in(seeds[9], part), 10)
    return {
        "activations": noise(part_keys[0], (ROWS, D), 1.0, 6.0, ((0, 2),)),
        "enc_weight": noise(part_keys[1], (D, LAT), D ** -0.5, 0.09375, ((0, 2), (1, 8)), jnp.float32),
        "dec_weight": noise(part_keys[2], (LAT, D), LAT ** -0.5, 0.0625, ((0, 8), (1, 2)), jnp.float32),
        "enc_bias": noise(part_keys[3], (LAT,), 0.5, 3.0, ((0, 8),), jnp.float32),
        "dec_bias": noise(part_keys[4], (D,), 0.5, 3.0, (), jnp.float32),
        "enc_first": noise(part_keys[5], (D, LAT), (0.3 / ROWS ** 0.5), 0.125, ((0, 2), (1, 8))),
        "enc_second": jnp.clip(jnp.exp(math.log(0.00019454956) - 4.6018058 * jax.random.uniform(part_keys[6], (D, LAT), jnp.float32) ** level_of(part_keys[6], (D, LAT), ((0, 2), (1, 8)), -0.2, 0.2)), 1.952052116394043e-06, 0.00019454956).astype(jnp.bfloat16),
        "dec_first": noise(part_keys[7], (LAT, D), (0.3 / ROWS ** 0.5), 0.125, ((0, 8), (1, 2))),
        "dec_second": jnp.clip(jnp.exp(math.log(0.00019454956) - 4.6018058 * jax.random.uniform(part_keys[8], (LAT, D), jnp.float32) ** level_of(part_keys[8], (LAT, D), ((0, 8), (1, 2)), -0.2, 0.2)), 1.952052116394043e-06, 0.00019454956).astype(jnp.bfloat16),
    }


l1_weight = 0.8
beta_one = 0.9
beta_two = 0.999
adam_eps = 1e-08
step_count = 1000.0

def adam_step(gradient, first, second):
    moment_one = beta_one * first.astype(jnp.float32) + (1.0 - beta_one) * gradient
    moment_two = beta_two * second.astype(jnp.float32) + (1.0 - beta_two) * gradient * gradient
    scaled_one = moment_one / (1.0 - beta_one ** step_count)
    scaled_two = moment_two / (1.0 - beta_two ** step_count)
    return (scaled_one / (jnp.sqrt(scaled_two) + adam_eps)).astype(jnp.bfloat16)

def reference(activations, enc_weight, dec_weight, enc_bias, dec_bias, enc_first, enc_second, dec_first, dec_second):
    total_rows = activations.shape[0]
    acts_full = activations.astype(jnp.float32)
    centered = (acts_full - dec_bias).astype(jnp.bfloat16)
    enc_low = enc_weight.astype(jnp.bfloat16)
    dec_low = dec_weight.astype(jnp.bfloat16)
    preact = jnp.dot(centered, enc_low, preferred_element_type=jnp.float32) + enc_bias
    latent_codes = jnp.maximum(preact, 0.0).astype(jnp.bfloat16)
    recon = jnp.dot(latent_codes, dec_low, preferred_element_type=jnp.float32) + dec_bias
    residual_grad = (2.0 / total_rows * (recon - acts_full)).astype(jnp.bfloat16)
    code_grad = jnp.dot(residual_grad, dec_low.T, preferred_element_type=jnp.float32) + l1_weight / total_rows
    pre_grad = jnp.where(preact > 0, code_grad, 0.0).astype(jnp.bfloat16)
    grad_dec = jnp.dot(latent_codes.T, residual_grad, preferred_element_type=jnp.float32)
    grad_enc = jnp.dot(centered.T, pre_grad, preferred_element_type=jnp.float32)
    return (adam_step(grad_enc, enc_first, enc_second), adam_step(grad_dec, dec_first, dec_second))
```

```python
import functools

import jax
import jax.numpy as jnp
from jax import lax
from jax.experimental import pallas as pl
from jax.experimental.pallas import tpu as pltpu
from jax.sharding import PartitionSpec as P

l1_weight = 0.8
beta_one = 0.9
beta_two = 0.999
adam_eps = 1e-08
step_count = 1000.0
subs = 4


def adam_step(gradient, first, second):
    moment_one = beta_one * first.astype(jnp.float32) + (1.0 - beta_one) * gradient
    moment_two = beta_two * second.astype(jnp.float32) + (1.0 - beta_two) * gradient * gradient
    scaled_one = moment_one / (1.0 - beta_one**step_count)
    scaled_two = moment_two / (1.0 - beta_two**step_count)
    return (scaled_one / (jnp.sqrt(scaled_two) + adam_eps)).astype(jnp.bfloat16)


def rows_product(left_rows, right_rows):
    return lax.dot_general(
        left_rows, right_rows, (((0,), (0,)), ((), ())), preferred_element_type=jnp.float32
    )


def ring_kernel(
    n,
    snake,
    total_rows,
    preact_ref,
    dec_own_ref,
    dec_peer_ref,
    bias_ref,
    acts_ref,
    pre_grad_ref,
    own_ref,
    recv_ref,
    dec,
    acts,
    sums,
    resid,
    codes,
    codes_t,
    code_grad,
    part,
    outgoing,
    rs_send,
    rs_recv,
    ag_send,
    ag_recv,
    x_send,
    x_recv,
    load_sem,
):
    rows, lats = preact_ref.shape
    width = resid.shape[2]
    half = n // 2
    sub_rows = rows // subs
    half_rows = rows // 2
    pieces = max(1, min(subs, lats // 256))
    piece = lats // pieces
    me = lax.axis_index("lat")
    row = lax.axis_index("row")

    def lat_of(pos):
        if not snake:
            return pos
        return jnp.where(pos < half, 2 * pos, 2 * (n - 1 - pos) + 1)

    if snake:
        pos = jnp.where(lax.rem(me, 2) == 0, me // 2, n - 1 - me // 2)
    else:
        pos = me
    targets = (lat_of(lax.rem(pos + 1, n)), lat_of(lax.rem(pos + n - 1, n)))

    barrier = pltpu.get_barrier_semaphore()
    for target in targets:
        pl.semaphore_signal(
            barrier, inc=1, device_id={"lat": target}, device_id_type=pl.DeviceIdType.MESH
        )
    pl.semaphore_signal(
        barrier, inc=1, device_id={"row": 1 - row}, device_id_type=pl.DeviceIdType.MESH
    )

    def shard_at(offset):
        return lax.rem(pos + offset + 2 * n, n)

    def columns(shard):
        return pl.ds(pl.multiple_of(lax.rem(shard, half) * width, width), width)

    load_own = pltpu.make_async_copy(dec_own_ref, dec.at[row], load_sem.at[0])
    load_peer = pltpu.make_async_copy(dec_peer_ref, dec.at[1 - row], load_sem.at[1])
    wide = pl.ds(pl.multiple_of(pos * width, width), width)
    load_acts = pltpu.make_async_copy(acts_ref.at[:, wide], acts, load_sem.at[2])
    load_own.start()
    load_peer.start()
    load_acts.start()
    codes[...] = jnp.maximum(preact_ref[...], 0.0).astype(jnp.bfloat16)
    load_own.wait()
    load_peer.wait()
    pl.semaphore_wait(barrier, 3)

    def dec_block(shard, lat_slice=slice(None)):
        return dec[shard // half, lat_slice, columns(shard)]

    def partial(way, shard):
        return jnp.dot(
            codes[pl.ds(way * half_rows, half_rows), :],
            dec_block(shard),
            preferred_element_type=jnp.float32,
        )

    def rs_copy(step, chain):
        return pltpu.make_async_remote_copy(
            src_ref=sums.at[step, chain],
            dst_ref=sums.at[step + 1, chain],
            send_sem=rs_send.at[step, chain],
            recv_sem=rs_recv.at[step, chain],
            device_id={"lat": targets[chain // 2]},
            device_id_type=pl.DeviceIdType.MESH,
        )

    def ag_copy(way, step, sub):
        shard = shard_at(-step if way == 0 else step)
        block = resid.at[shard, pl.ds(sub * sub_rows, sub_rows), :]
        return pltpu.make_async_remote_copy(
            src_ref=block,
            dst_ref=block,
            send_sem=ag_send.at[way, step, sub],
            recv_sem=ag_recv.at[way, step, sub],
            device_id={"lat": targets[way]},
            device_id_type=pl.DeviceIdType.MESH,
        )

    def exchange(block):
        place = pl.ds(pl.multiple_of(block * width, width), width)
        return pltpu.make_async_remote_copy(
            src_ref=outgoing.at[block],
            dst_ref=recv_ref.at[:, place],
            send_sem=x_send.at[block],
            recv_sem=x_recv.at[block],
            device_id={"row": 1 - row},
            device_id_type=pl.DeviceIdType.MESH,
        )

    for way in range(2):
        first = partial(way, shard_at(-1 if way == 0 else 1))
        for sub in range(2):
            chain = way * 2 + sub
            sums[0, chain] = first[sub * sub_rows : (sub + 1) * sub_rows].astype(jnp.bfloat16)
            rs_copy(0, chain).start()
    codes_t[...] = jnp.maximum(jnp.transpose(preact_ref[...]), 0.0).astype(jnp.bfloat16)

    def own_term(way, sub):
        return part[way, pl.ds(sub * sub_rows, sub_rows), :]

    @pl.loop(1, n - 1)
    def _(step):
        for way in range(2):
            part[way] = partial(way, shard_at(-1 - step if way == 0 else 1 + step))
        for sub in range(2):
            for way in range(2):
                chain = way * 2 + sub
                rs_copy(step - 1, chain).wait_recv()
                sums[step, chain] = (
                    sums[step, chain].astype(jnp.float32) + own_term(way, sub)
                ).astype(jnp.bfloat16)
                rs_copy(step, chain).start()

    for way in range(2):
        part[way] = partial(way, pos)
    load_acts.wait()
    for sub in range(2):
        for way in range(2):
            chain = way * 2 + sub
            rs_copy(n - 2, chain).wait_recv()
            recon = sums[n - 1, chain].astype(jnp.float32) + own_term(way, sub) + bias_ref[:, wide]
            target_rows = pl.ds(chain * sub_rows, sub_rows)
            resid[pos, target_rows, :] = (
                2.0 / total_rows * (recon - acts[target_rows, :].astype(jnp.float32))
            ).astype(jnp.bfloat16)
            ag_copy(0, 0, chain).start()
            ag_copy(1, 0, chain).start()

    def compute(shard, sub, fresh=False):
        if sub >= pieces:
            return
        lat_slice = pl.ds(sub * piece, piece)
        block = resid[shard]
        term = lax.dot_general(
            block,
            dec_block(shard, lat_slice),
            (((1,), (1,)), ((), ())),
            preferred_element_type=jnp.float32,
        )
        if fresh:
            code_grad[:, lat_slice] = term
        else:
            code_grad[:, lat_slice] += term
        grad = jnp.dot(
            codes_t[lat_slice, :], block, preferred_element_type=jnp.float32
        ).astype(jnp.bfloat16)
        mine = shard // half == row

        @pl.when(mine)
        def _():
            own_ref[lat_slice, columns(shard)] = grad

        @pl.when(jnp.logical_not(mine))
        def _():
            outgoing[lax.rem(shard, half), lat_slice, :] = grad
            if sub == pieces - 1:
                exchange(lax.rem(shard, half)).start()

    def forward(step, sub):
        for way in range(2):
            ag_copy(way, step, sub).wait_recv()
            if sub // 2 == way:
                ag_copy(way, step + 1, sub).start()
            else:

                @pl.when(step < half - 2)
                def _():
                    ag_copy(way, step + 1, sub).start()

    for sub in range(subs):
        compute(pos, sub, fresh=True)
        forward(0, sub)

    @pl.loop(1, half - 1)
    def _(step):
        for sub in range(subs):
            compute(shard_at(-step), sub)
            compute(shard_at(step), sub)
            forward(step, sub)

    for sub in range(subs):
        compute(shard_at(1 - half), sub)
        compute(shard_at(half - 1), sub)
    for sub in range(subs):
        ag_copy(sub // 2, half - 1, sub).wait_recv()
    for sub in range(subs):
        compute(shard_at(half), sub)
    pre_grad_ref[...] = jnp.where(
        preact_ref[...] > 0, code_grad[...] + l1_weight / total_rows, 0.0
    ).astype(jnp.bfloat16)

    @pl.loop(0, n - 1)
    def _(step):
        for chain in range(subs):
            rs_copy(step, chain).wait_send()

    @pl.loop(0, half - 1)
    def _(step):
        for way in range(2):
            for sub in range(subs):
                ag_copy(way, step, sub).wait_send()

    for sub in range(subs):
        ag_copy(sub // 2, half - 1, sub).wait_send()

    @pl.loop(0, half)
    def _(block):
        exchange(block).wait_send()
        exchange(block).wait_recv()


def residual_step(preact, dec_own, dec_peer, dec_bias, activations, total_rows):
    n = lax.axis_size("lat")
    rows, lats = preact.shape
    model = activations.shape[1]
    width = model // n
    half = n // 2
    bf16, f32 = jnp.bfloat16, jnp.float32
    vmem = pl.BlockSpec(memory_space=pltpu.VMEM)
    whole = pl.BlockSpec(memory_space=pl.ANY)
    return pl.pallas_call(
        functools.partial(ring_kernel, n, n <= 8, total_rows),
        out_shape=(
            jax.ShapeDtypeStruct((rows, lats), bf16),
            jax.ShapeDtypeStruct((lats, model // 2), bf16),
            jax.ShapeDtypeStruct((lats, model // 2), bf16),
        ),
        in_specs=[vmem, whole, whole, vmem, whole],
        out_specs=(vmem, vmem, vmem),
        scratch_shapes=[
            pltpu.VMEM((2, lats, model // 2), bf16),
            pltpu.VMEM((rows, width), bf16),
            pltpu.VMEM((n, subs, rows // subs, width), bf16),
            pltpu.VMEM((n, rows, width), bf16),
            pltpu.VMEM((rows, lats), bf16),
            pltpu.VMEM((lats, rows), bf16),
            pltpu.VMEM((rows, lats), f32),
            pltpu.VMEM((2, rows // 2, width), f32),
            pltpu.VMEM((half, lats, width), bf16),
            pltpu.SemaphoreType.DMA((n - 1, subs)),
            pltpu.SemaphoreType.DMA((n - 1, subs)),
            pltpu.SemaphoreType.DMA((2, half, subs)),
            pltpu.SemaphoreType.DMA((2, half, subs)),
            pltpu.SemaphoreType.DMA((half,)),
            pltpu.SemaphoreType.DMA((half,)),
            pltpu.SemaphoreType.DMA((3,)),
        ],
        compiler_params=pltpu.CompilerParams(
            collective_id=0, has_side_effects=True, vmem_limit_bytes=58 * 1024 * 1024
        ),
        cost_estimate=pl.CostEstimate(
            flops=6 * rows * lats * model, bytes_accessed=30 * 1024 * 1024, transcendentals=0
        ),
    )(preact, dec_own, dec_peer, dec_bias.reshape(1, -1), activations)


def on_device(
    activations,
    enc_weight,
    dec_weight,
    enc_bias,
    dec_bias,
    enc_first,
    enc_second,
    dec_first,
    dec_second,
):
    total_rows = activations.shape[0] * lax.axis_size("row")
    row = lax.axis_index("row")
    part = enc_weight.shape[0]
    swap = [(0, 1), (1, 0)]
    enc_low = enc_weight.astype(jnp.bfloat16)
    enc_peer = lax.ppermute(enc_low, "row", swap)
    dec_low = dec_weight.astype(jnp.bfloat16)
    dec_peer = lax.ppermute(dec_low, "row", swap)

    centered = (activations.astype(jnp.float32) - dec_bias).astype(jnp.bfloat16)
    centered_own = lax.dynamic_slice_in_dim(centered, row * part, part, 1)
    centered_peer = lax.dynamic_slice_in_dim(centered, (1 - row) * part, part, 1)
    preact = jnp.dot(centered_own, enc_low, preferred_element_type=jnp.float32)
    preact = preact + jnp.dot(centered_peer, enc_peer, preferred_element_type=jnp.float32)
    preact = preact + enc_bias

    pre_grad, grad_dec_own, grad_dec_peer = residual_step(
        preact, dec_low, dec_peer, dec_bias, activations, total_rows
    )
    grad_out = rows_product(centered_peer, pre_grad).astype(jnp.bfloat16)
    grad_in = lax.ppermute(grad_out, "row", swap)
    dec_step = adam_step(
        grad_dec_own.astype(jnp.float32) + grad_dec_peer.astype(jnp.float32), dec_first, dec_second
    )
    grad_enc = rows_product(centered_own, pre_grad) + grad_in.astype(jnp.float32)
    return (adam_step(grad_enc, enc_first, enc_second), dec_step)


def solution(mesh):
    return jax.shard_map(
        on_device,
        mesh=mesh,
        in_specs=(
            P(("grp", "row"), None),
            P(("grp", "row"), "lat"),
            P(("grp", "lat"), "row"),
            P(("grp", "lat")),
            P("grp"),
            P(("grp", "row"), "lat"),
            P(("grp", "row"), "lat"),
            P(("grp", "lat"), "row"),
            P(("grp", "lat"), "row"),
        ),
        out_specs=(P(("grp", "row"), "lat"), P(("grp", "lat"), "row")),
        check_vma=False,
    )
```

```python
import functools

import jax
import jax.numpy as jnp
from jax import lax
from jax.experimental import pallas as pl
from jax.experimental.pallas import tpu as pltpu
from jax.sharding import PartitionSpec as P

l1_weight = 0.8
beta_one = 0.9
beta_two = 0.999
adam_eps = 1e-08
step_count = 1000.0
subs = 4
blocks = 8


def adam_step(gradient, first, second):
    moment_one = beta_one * first.astype(jnp.float32) + (1.0 - beta_one) * gradient
    moment_two = beta_two * second.astype(jnp.float32) + (1.0 - beta_two) * gradient * gradient
    scaled_one = moment_one / (1.0 - beta_one**step_count)
    scaled_two = moment_two / (1.0 - beta_two**step_count)
    return (scaled_one / (jnp.sqrt(scaled_two) + adam_eps)).astype(jnp.bfloat16)


def rows_product(left_rows, right_rows):
    return lax.dot_general(
        left_rows, right_rows, (((0,), (0,)), ((), ())), preferred_element_type=jnp.float32
    )


def ring_kernel(
    n,
    snake,
    total_rows,
    enc_ref,
    dec_ref,
    enc_bias_ref,
    bias_ref,
    acts_ref,
    pre_grad_ref,
    own_ref,
    recv_ref,
    centered_ref,
    preact,
    centered,
    enc,
    enc_stage,
    dec_stage,
    dec,
    acts,
    sums,
    resid,
    codes,
    codes_t,
    code_grad,
    part,
    outgoing,
    rs_send,
    rs_recv,
    ag_send,
    ag_recv,
    x_send,
    x_recv,
    load_sem,
    enc_load,
    dec_load,
    enc_send,
    enc_recv,
    dec_send,
    dec_recv,
    keep_sem,
):
    rows, lats = preact.shape
    width = resid.shape[2]
    half = n // 2
    sub_rows = rows // subs
    half_rows = rows // 2
    pieces = max(1, min(subs, lats // 256))
    piece = lats // pieces
    me = lax.axis_index("lat")
    row = lax.axis_index("row")

    def lat_of(pos):
        if not snake:
            return pos
        return jnp.where(pos < half, 2 * pos, 2 * (n - 1 - pos) + 1)

    if snake:
        pos = jnp.where(lax.rem(me, 2) == 0, me // 2, n - 1 - me // 2)
    else:
        pos = me
    targets = (lat_of(lax.rem(pos + 1, n)), lat_of(lax.rem(pos + n - 1, n)))

    barrier = pltpu.get_barrier_semaphore()
    for target in targets:
        pl.semaphore_signal(
            barrier, inc=1, device_id={"lat": target}, device_id_type=pl.DeviceIdType.MESH
        )
    pl.semaphore_signal(
        barrier, inc=1, device_id={"row": 1 - row}, device_id_type=pl.DeviceIdType.MESH
    )

    def shard_at(offset):
        return lax.rem(pos + offset + 2 * n, n)

    def columns(shard):
        return pl.ds(pl.multiple_of(lax.rem(shard, half) * width, width), width)

    wide = pl.ds(pl.multiple_of(pos * width, width), width)
    load_acts = pltpu.make_async_copy(acts_ref.at[:, wide], acts, load_sem.at[0])
    load_all = pltpu.make_async_copy(acts_ref, centered, load_sem.at[1])
    save_centered = pltpu.make_async_copy(centered, centered_ref, load_sem.at[2])
    enc_rows = enc_stage.shape[1]
    dec_rows = dec_stage.shape[1]
    model_half = enc_ref.shape[0]

    def load_enc(block):
        return pltpu.make_async_copy(
            enc_ref.at[pl.ds(block * enc_rows, enc_rows), :],
            enc_stage.at[lax.rem(block, 2)],
            enc_load.at[lax.rem(block, 2)],
        )

    def load_dec(block):
        return pltpu.make_async_copy(
            dec_ref.at[pl.ds(block * dec_rows, dec_rows), :],
            dec_stage.at[lax.rem(block, 2)],
            dec_load.at[lax.rem(block, 2)],
        )

    def swap_enc(block):
        place = enc.at[row, pl.ds(block * enc_rows, enc_rows), :]
        return pltpu.make_async_remote_copy(
            src_ref=place,
            dst_ref=place,
            send_sem=enc_send.at[block],
            recv_sem=enc_recv.at[block],
            device_id={"row": 1 - row},
            device_id_type=pl.DeviceIdType.MESH,
        )

    def swap_dec(block):
        place = dec.at[row, pl.ds(block * dec_rows, dec_rows), :]
        return pltpu.make_async_remote_copy(
            src_ref=place,
            dst_ref=place,
            send_sem=dec_send.at[block],
            recv_sem=dec_recv.at[block],
            device_id={"row": 1 - row},
            device_id_type=pl.DeviceIdType.MESH,
        )

    load_all.start()
    load_enc(0).start()
    load_enc(1).start()
    load_dec(0).start()
    load_dec(1).start()
    load_acts.start()
    preact[...] = jnp.broadcast_to(enc_bias_ref[...], preact.shape)
    pl.semaphore_wait(barrier, 3)
    load_all.wait()

    def encode(owner, block):
        place = pl.ds(pl.multiple_of(owner * model_half + block * enc_rows, enc_rows), enc_rows)
        chunk = (centered[:, place].astype(jnp.float32) - bias_ref[:, place]).astype(jnp.bfloat16)
        centered[:, place] = chunk
        preact[...] += jnp.dot(
            chunk,
            enc[owner, pl.ds(block * enc_rows, enc_rows), :],
            preferred_element_type=jnp.float32,
        )

    @pl.loop(0, blocks)
    def _(block):
        load_enc(block).wait()
        enc[row, pl.ds(block * enc_rows, enc_rows), :] = enc_stage[lax.rem(block, 2)].astype(
            jnp.bfloat16
        )
        swap_enc(block).start()

        @pl.when(block < blocks - 2)
        def _():
            load_enc(block + 2).start()

        load_dec(block).wait()
        dec[row, pl.ds(block * dec_rows, dec_rows), :] = dec_stage[lax.rem(block, 2)].astype(
            jnp.bfloat16
        )
        swap_dec(block).start()

        @pl.when(block < blocks - 2)
        def _():
            load_dec(block + 2).start()

        encode(row, block)

    @pl.loop(0, blocks)
    def _(block):
        swap_enc(block).wait_recv()
        encode(1 - row, block)

    save_centered.start()
    codes[...] = jnp.maximum(preact[...], 0.0).astype(jnp.bfloat16)

    @pl.loop(0, blocks)
    def _(block):
        swap_dec(block).wait_recv()

    def dec_block(shard, lat_slice=slice(None)):
        return dec[shard // half, lat_slice, columns(shard)]

    def partial(way, shard):
        return jnp.dot(
            codes[pl.ds(way * half_rows, half_rows), :],
            dec_block(shard),
            preferred_element_type=jnp.float32,
        )

    def rs_copy(step, chain):
        return pltpu.make_async_remote_copy(
            src_ref=sums.at[step, chain],
            dst_ref=sums.at[step + 1, chain],
            send_sem=rs_send.at[step, chain],
            recv_sem=rs_recv.at[step, chain],
            device_id={"lat": targets[chain // 2]},
            device_id_type=pl.DeviceIdType.MESH,
        )

    def ag_copy(way, step, sub):
        shard = shard_at(-step if way == 0 else step)
        block = resid.at[shard, pl.ds(sub * sub_rows, sub_rows), :]
        return pltpu.make_async_remote_copy(
            src_ref=block,
            dst_ref=block,
            send_sem=ag_send.at[way, step, sub],
            recv_sem=ag_recv.at[way, step, sub],
            device_id={"lat": targets[way]},
            device_id_type=pl.DeviceIdType.MESH,
        )

    def exchange(block):
        place = pl.ds(pl.multiple_of(block * width, width), width)
        return pltpu.make_async_remote_copy(
            src_ref=outgoing.at[(1 - row) * half + block],
            dst_ref=recv_ref.at[:, place],
            send_sem=x_send.at[block],
            recv_sem=x_recv.at[block],
            device_id={"row": 1 - row},
            device_id_type=pl.DeviceIdType.MESH,
        )

    def keep(block):
        place = pl.ds(pl.multiple_of(block * width, width), width)
        return pltpu.make_async_copy(
            outgoing.at[row * half + block], own_ref.at[:, place], keep_sem.at[block]
        )

    for way in range(2):
        first = partial(way, shard_at(-1 if way == 0 else 1))
        for sub in range(2):
            chain = way * 2 + sub
            sums[0, chain] = first[sub * sub_rows : (sub + 1) * sub_rows].astype(jnp.bfloat16)
            rs_copy(0, chain).start()
    codes_t[...] = jnp.maximum(jnp.transpose(preact[...]), 0.0).astype(jnp.bfloat16)

    def own_term(way, sub):
        return part[way, pl.ds(sub * sub_rows, sub_rows), :]

    @pl.loop(1, n - 1)
    def _(step):
        for way in range(2):
            part[way] = partial(way, shard_at(-1 - step if way == 0 else 1 + step))
        for sub in range(2):
            for way in range(2):
                chain = way * 2 + sub
                rs_copy(step - 1, chain).wait_recv()
                sums[step, chain] = (
                    sums[step, chain].astype(jnp.float32) + own_term(way, sub)
                ).astype(jnp.bfloat16)
                rs_copy(step, chain).start()

    for way in range(2):
        part[way] = partial(way, pos)
    load_acts.wait()
    for sub in range(2):
        for way in range(2):
            chain = way * 2 + sub
            rs_copy(n - 2, chain).wait_recv()
            recon = sums[n - 1, chain].astype(jnp.float32) + own_term(way, sub) + bias_ref[:, wide]
            target_rows = pl.ds(chain * sub_rows, sub_rows)
            resid[pos, target_rows, :] = (
                2.0 / total_rows * (recon - acts[target_rows, :].astype(jnp.float32))
            ).astype(jnp.bfloat16)
            ag_copy(0, 0, chain).start()
            ag_copy(1, 0, chain).start()

    def compute(shard, sub, fresh=False):
        if sub >= pieces:
            return
        lat_slice = pl.ds(sub * piece, piece)
        block = resid[shard]
        term = lax.dot_general(
            block,
            dec_block(shard, lat_slice),
            (((1,), (1,)), ((), ())),
            preferred_element_type=jnp.float32,
        )
        if fresh:
            code_grad[:, lat_slice] = term
        else:
            code_grad[:, lat_slice] += term
        grad = jnp.dot(
            codes_t[lat_slice, :], block, preferred_element_type=jnp.float32
        ).astype(jnp.bfloat16)
        outgoing[shard, lat_slice, :] = grad
        if sub == pieces - 1:
            mine = shard // half == row

            @pl.when(mine)
            def _():
                keep(lax.rem(shard, half)).start()

            @pl.when(jnp.logical_not(mine))
            def _():
                exchange(lax.rem(shard, half)).start()

    def forward(step, sub):
        for way in range(2):
            ag_copy(way, step, sub).wait_recv()
            if sub // 2 == way:
                ag_copy(way, step + 1, sub).start()
            else:

                @pl.when(step < half - 2)
                def _():
                    ag_copy(way, step + 1, sub).start()

    for sub in range(subs):
        compute(pos, sub, fresh=True)
        forward(0, sub)

    @pl.loop(1, half - 1)
    def _(step):
        for sub in range(subs):
            compute(shard_at(-step), sub)
            compute(shard_at(step), sub)
            forward(step, sub)

    for sub in range(subs):
        compute(shard_at(1 - half), sub)
        compute(shard_at(half - 1), sub)
    for sub in range(subs):
        ag_copy(sub // 2, half - 1, sub).wait_recv()
    for sub in range(subs):
        compute(shard_at(half), sub)
    pre_grad_ref[...] = jnp.where(
        preact[...] > 0, code_grad[...] + l1_weight / total_rows, 0.0
    ).astype(jnp.bfloat16)

    @pl.loop(0, n - 1)
    def _(step):
        for chain in range(subs):
            rs_copy(step, chain).wait_send()

    @pl.loop(0, half - 1)
    def _(step):
        for way in range(2):
            for sub in range(subs):
                ag_copy(way, step, sub).wait_send()

    for sub in range(subs):
        ag_copy(sub // 2, half - 1, sub).wait_send()

    @pl.loop(0, half)
    def _(block):
        exchange(block).wait_send()
        exchange(block).wait_recv()
        keep(block).wait()

    @pl.loop(0, blocks)
    def _(block):
        swap_enc(block).wait_send()
        swap_dec(block).wait_send()

    save_centered.wait()


def residual_step(enc_weight, dec_weight, enc_bias, dec_bias, activations, total_rows):
    n = lax.axis_size("lat")
    rows, model = activations.shape
    lats = enc_weight.shape[1]
    width = model // n
    half = n // 2
    bf16, f32 = jnp.bfloat16, jnp.float32
    vmem = pl.BlockSpec(memory_space=pltpu.VMEM)
    whole = pl.BlockSpec(memory_space=pl.ANY)
    return pl.pallas_call(
        functools.partial(ring_kernel, n, n <= 8, total_rows),
        out_shape=(
            jax.ShapeDtypeStruct((rows, lats), bf16),
            jax.ShapeDtypeStruct((lats, model // 2), bf16),
            jax.ShapeDtypeStruct((lats, model // 2), bf16),
            jax.ShapeDtypeStruct((rows, model), bf16),
        ),
        in_specs=[whole, whole, vmem, vmem, whole],
        out_specs=(vmem, whole, whole, whole),
        scratch_shapes=[
            pltpu.VMEM((rows, lats), f32),
            pltpu.VMEM((rows, model), bf16),
            pltpu.VMEM((2, model // 2, lats), bf16),
            pltpu.VMEM((2, model // 2 // blocks, lats), f32),
            pltpu.VMEM((2, lats // blocks, model // 2), f32),
            pltpu.VMEM((2, lats, model // 2), bf16),
            pltpu.VMEM((rows, width), bf16),
            pltpu.VMEM((n, subs, rows // subs, width), bf16),
            pltpu.VMEM((n, rows, width), bf16),
            pltpu.VMEM((rows, lats), bf16),
            pltpu.VMEM((lats, rows), bf16),
            pltpu.VMEM((rows, lats), f32),
            pltpu.VMEM((2, rows // 2, width), f32),
            pltpu.VMEM((n, lats, width), bf16),
            pltpu.SemaphoreType.DMA((n - 1, subs)),
            pltpu.SemaphoreType.DMA((n - 1, subs)),
            pltpu.SemaphoreType.DMA((2, half, subs)),
            pltpu.SemaphoreType.DMA((2, half, subs)),
            pltpu.SemaphoreType.DMA((half,)),
            pltpu.SemaphoreType.DMA((half,)),
            pltpu.SemaphoreType.DMA((3,)),
            pltpu.SemaphoreType.DMA((2,)),
            pltpu.SemaphoreType.DMA((2,)),
            pltpu.SemaphoreType.DMA((blocks,)),
            pltpu.SemaphoreType.DMA((blocks,)),
            pltpu.SemaphoreType.DMA((blocks,)),
            pltpu.SemaphoreType.DMA((blocks,)),
            pltpu.SemaphoreType.DMA((half,)),
        ],
        compiler_params=pltpu.CompilerParams(
            collective_id=0, has_side_effects=True, vmem_limit_bytes=60 * 1024 * 1024
        ),
        cost_estimate=pl.CostEstimate(
            flops=8 * rows * lats * model, bytes_accessed=30 * 1024 * 1024, transcendentals=0
        ),
    )(enc_weight, dec_weight, enc_bias.reshape(1, -1), dec_bias.reshape(1, -1), activations)


def on_device(
    activations,
    enc_weight,
    dec_weight,
    enc_bias,
    dec_bias,
    enc_first,
    enc_second,
    dec_first,
    dec_second,
):
    total_rows = activations.shape[0] * lax.axis_size("row")
    row = lax.axis_index("row")
    part = enc_weight.shape[0]
    swap = [(0, 1), (1, 0)]
    pre_grad, grad_dec_own, grad_dec_peer, centered = residual_step(
        enc_weight, dec_weight, enc_bias, dec_bias, activations, total_rows
    )
    centered_own = lax.dynamic_slice_in_dim(centered, row * part, part, 1)
    centered_peer = lax.dynamic_slice_in_dim(centered, (1 - row) * part, part, 1)
    grad_out = rows_product(centered_peer, pre_grad).astype(jnp.bfloat16)
    grad_in = lax.ppermute(grad_out, "row", swap)
    dec_step = adam_step(
        grad_dec_own.astype(jnp.float32) + grad_dec_peer.astype(jnp.float32), dec_first, dec_second
    )
    grad_enc = rows_product(centered_own, pre_grad) + grad_in.astype(jnp.float32)
    return (adam_step(grad_enc, enc_first, enc_second), dec_step)


def solution(mesh):
    return jax.shard_map(
        on_device,
        mesh=mesh,
        in_specs=(
            P(("grp", "row"), None),
            P(("grp", "row"), "lat"),
            P(("grp", "lat"), "row"),
            P(("grp", "lat")),
            P("grp"),
            P(("grp", "row"), "lat"),
            P(("grp", "row"), "lat"),
            P(("grp", "lat"), "row"),
            P(("grp", "lat"), "row"),
        ),
        out_specs=(P(("grp", "row"), "lat"), P(("grp", "lat"), "row")),
        check_vma=False,
    )
```

```python
import functools

import jax
import jax.numpy as jnp
from jax import lax
from jax.experimental import pallas as pl
from jax.experimental.pallas import tpu as pltpu
from jax.sharding import PartitionSpec as P

l1_weight = 0.8
beta_one = 0.9
beta_two = 0.999
adam_eps = 1e-08
step_count = 1000.0
subs = 4
blocks = 8
chunk_rows = 32


def adam_step(gradient, first, second):
    moment_one = beta_one * first.astype(jnp.float32) + (1.0 - beta_one) * gradient
    moment_two = beta_two * second.astype(jnp.float32) + (1.0 - beta_two) * gradient * gradient
    scaled_one = moment_one / (1.0 - beta_one**step_count)
    scaled_two = moment_two / (1.0 - beta_two**step_count)
    return (scaled_one / (jnp.sqrt(scaled_two) + adam_eps)).astype(jnp.bfloat16)


def rows_product(left_rows, right_rows):
    return lax.dot_general(
        left_rows, right_rows, (((0,), (0,)), ((), ())), preferred_element_type=jnp.float32
    )


def ring_kernel(
    n,
    snake,
    total_rows,
    enc_ref,
    dec_ref,
    enc_bias_ref,
    bias_ref,
    acts_ref,
    first_ref,
    second_ref,
    pre_grad_ref,
    step_ref,
    centered_ref,
    preact,
    centered,
    enc,
    enc_stage,
    dec_stage,
    dec,
    acts,
    sums,
    resid,
    codes,
    codes_t,
    code_grad,
    part,
    outgoing,
    rs_send,
    rs_recv,
    ag_send,
    ag_recv,
    x_send,
    x_recv,
    load_sem,
    enc_load,
    dec_load,
    enc_send,
    enc_recv,
    dec_send,
    dec_recv,
    keep_sem,
    moment_sem,
    arrived,
):
    rows, lats = preact.shape
    width = resid.shape[2]
    half = n // 2
    sub_rows = rows // subs
    half_rows = rows // 2
    pieces = max(1, min(subs, lats // 256))
    piece = lats // pieces
    me = lax.axis_index("lat")
    row = lax.axis_index("row")

    def lat_of(pos):
        if not snake:
            return pos
        return jnp.where(pos < half, 2 * pos, 2 * (n - 1 - pos) + 1)

    if snake:
        pos = jnp.where(lax.rem(me, 2) == 0, me // 2, n - 1 - me // 2)
    else:
        pos = me
    targets = (lat_of(lax.rem(pos + 1, n)), lat_of(lax.rem(pos + n - 1, n)))

    barrier = pltpu.get_barrier_semaphore()
    for target in targets:
        pl.semaphore_signal(
            barrier, inc=1, device_id={"lat": target}, device_id_type=pl.DeviceIdType.MESH
        )
    pl.semaphore_signal(
        barrier, inc=1, device_id={"row": 1 - row}, device_id_type=pl.DeviceIdType.MESH
    )

    def shard_at(offset):
        return lax.rem(pos + offset + 2 * n, n)

    def columns(shard):
        return pl.ds(pl.multiple_of(shard // 2 * width, width), width)

    wide = pl.ds(
        pl.multiple_of(lax.rem(pos, 2) * enc_ref.shape[0] + pos // 2 * width, width), width
    )
    load_acts = pltpu.make_async_copy(acts_ref.at[:, wide], acts, load_sem.at[0])
    load_all = pltpu.make_async_copy(acts_ref, centered, load_sem.at[1])
    save_centered = pltpu.make_async_copy(centered, centered_ref, load_sem.at[2])
    enc_rows = enc_stage.shape[1]
    dec_rows = dec_stage.shape[1]
    model_half = enc_ref.shape[0]

    def load_enc(block):
        return pltpu.make_async_copy(
            enc_ref.at[pl.ds(block * enc_rows, enc_rows), :],
            enc_stage.at[lax.rem(block, 2)],
            enc_load.at[lax.rem(block, 2)],
        )

    def load_dec(block):
        return pltpu.make_async_copy(
            dec_ref.at[pl.ds(block * dec_rows, dec_rows), :],
            dec_stage.at[lax.rem(block, 2)],
            dec_load.at[lax.rem(block, 2)],
        )

    def swap_enc(block):
        place = enc.at[row, pl.ds(block * enc_rows, enc_rows), :]
        return pltpu.make_async_remote_copy(
            src_ref=place,
            dst_ref=place,
            send_sem=enc_send.at[block],
            recv_sem=enc_recv.at[block],
            device_id={"row": 1 - row},
            device_id_type=pl.DeviceIdType.MESH,
        )

    def swap_dec(block):
        place = dec.at[row, pl.ds(block * dec_rows, dec_rows), :]
        return pltpu.make_async_remote_copy(
            src_ref=place,
            dst_ref=place,
            send_sem=dec_send.at[block],
            recv_sem=dec_recv.at[block],
            device_id={"row": 1 - row},
            device_id_type=pl.DeviceIdType.MESH,
        )

    load_all.start()
    load_enc(0).start()
    load_enc(1).start()
    load_dec(0).start()
    load_dec(1).start()
    load_acts.start()
    preact[...] = jnp.broadcast_to(enc_bias_ref[...], preact.shape)
    pl.semaphore_wait(barrier, 3)
    load_all.wait()

    def encode(owner, block):
        place = pl.ds(pl.multiple_of(owner * model_half + block * enc_rows, enc_rows), enc_rows)
        chunk = (centered[:, place].astype(jnp.float32) - bias_ref[:, place]).astype(jnp.bfloat16)
        centered[:, place] = chunk
        preact[...] += jnp.dot(
            chunk,
            enc[owner, pl.ds(block * enc_rows, enc_rows), :],
            preferred_element_type=jnp.float32,
        )

    @pl.loop(0, blocks)
    def _(block):
        load_enc(block).wait()
        enc[row, pl.ds(block * enc_rows, enc_rows), :] = enc_stage[lax.rem(block, 2)].astype(
            jnp.bfloat16
        )
        swap_enc(block).start()

        @pl.when(block < blocks - 2)
        def _():
            load_enc(block + 2).start()

        for piece_of in range(2):
            lower = 2 * block + piece_of
            load_dec(lower).wait()
            dec[row, pl.ds(lower * dec_rows, dec_rows), :] = dec_stage[piece_of].astype(
                jnp.bfloat16
            )
            swap_dec(lower).start()

            @pl.when(block < blocks - 1)
            def _():
                load_dec(lower + 2).start()

        encode(row, block)

    @pl.loop(0, blocks)
    def _(block):
        swap_enc(block).wait_recv()
        encode(1 - row, block)

    save_centered.start()
    codes[...] = jnp.maximum(preact[...], 0.0).astype(jnp.bfloat16)

    @pl.loop(0, 2 * blocks)
    def _(block):
        swap_dec(block).wait_recv()

    def dec_block(shard, lat_slice=slice(None)):
        return dec[lax.rem(shard, 2), lat_slice, columns(shard)]

    def partial(way, shard):
        return jnp.dot(
            codes[pl.ds(way * half_rows, half_rows), :],
            dec_block(shard),
            preferred_element_type=jnp.float32,
        )

    def rs_copy(step, chain):
        return pltpu.make_async_remote_copy(
            src_ref=sums.at[step, chain],
            dst_ref=sums.at[step + 1, chain],
            send_sem=rs_send.at[step, chain],
            recv_sem=rs_recv.at[step, chain],
            device_id={"lat": targets[chain // 2]},
            device_id_type=pl.DeviceIdType.MESH,
        )

    def ag_copy(way, step, sub):
        shard = shard_at(-step if way == 0 else step)
        block = resid.at[shard, pl.ds(sub * sub_rows, sub_rows), :]
        return pltpu.make_async_remote_copy(
            src_ref=block,
            dst_ref=block,
            send_sem=ag_send.at[way, step, sub],
            recv_sem=ag_recv.at[way, step, sub],
            device_id={"lat": targets[way]},
            device_id_type=pl.DeviceIdType.MESH,
        )

    def exchange(block):
        return pltpu.make_async_remote_copy(
            src_ref=outgoing.at[2 * block + 1 - row],
            dst_ref=arrived.at[block],
            send_sem=x_send.at[block],
            recv_sem=x_recv.at[block],
            device_id={"row": 1 - row},
            device_id_type=pl.DeviceIdType.MESH,
        )

    def keep(block):
        place = pl.ds(pl.multiple_of(block * width, width), width)
        return pltpu.make_async_copy(
            outgoing.at[2 * block + row], step_ref.at[:, place], keep_sem.at[block]
        )

    across = lats // width

    def moment_place(block, start, size):
        return (
            pl.ds(pl.multiple_of(block // across * lats + start, chunk_rows), size),
            pl.ds(pl.multiple_of(lax.rem(block, across) * width, width), width),
        )

    def load_moment(which, block):
        source = (first_ref, second_ref)[which]
        place = pl.ds(pl.multiple_of(block * width, width), width)
        down, along = moment_place(block, 0, lats)
        return pltpu.make_async_copy(
            source.at[:, place], enc.at[which, down, along], moment_sem.at[which, block]
        )

    @pl.loop(0, blocks)
    def _(block):
        swap_enc(block).wait_send()

    @pl.loop(0, half)
    def _(block):
        load_moment(0, block).start()
        load_moment(1, block).start()

    def adam_block(shard):
        block = shard // 2

        @pl.when(lax.rem(shard, 2) == row)
        def _():
            load_moment(0, block).wait()
            load_moment(1, block).wait()
            exchange(block).wait_recv()

            @pl.loop(0, lats // chunk_rows)
            def _(chunk):
                start = pl.multiple_of(chunk * chunk_rows, chunk_rows)
                lines = pl.ds(start, chunk_rows)
                down, along = moment_place(block, start, chunk_rows)
                grad = outgoing[shard, lines, :].astype(jnp.float32)
                grad = grad + arrived[block, lines, :].astype(jnp.float32)
                outgoing[shard, lines, :] = adam_step(
                    grad, enc[0, down, along], enc[1, down, along]
                )

            keep(block).start()

    for way in range(2):
        first = partial(way, shard_at(-1 if way == 0 else 1))
        for sub in range(2):
            chain = way * 2 + sub
            sums[0, chain] = first[sub * sub_rows : (sub + 1) * sub_rows].astype(jnp.bfloat16)
            rs_copy(0, chain).start()
    codes_t[...] = jnp.maximum(jnp.transpose(preact[...]), 0.0).astype(jnp.bfloat16)

    def own_term(way, sub):
        return part[way, pl.ds(sub * sub_rows, sub_rows), :]

    @pl.loop(1, n - 1)
    def _(step):
        for way in range(2):
            part[way] = partial(way, shard_at(-1 - step if way == 0 else 1 + step))
        for sub in range(2):
            for way in range(2):
                chain = way * 2 + sub
                rs_copy(step - 1, chain).wait_recv()
                sums[step, chain] = (
                    sums[step, chain].astype(jnp.float32) + own_term(way, sub)
                ).astype(jnp.bfloat16)
                rs_copy(step, chain).start()

    for way in range(2):
        part[way] = partial(way, pos)
    load_acts.wait()
    for sub in range(2):
        for way in range(2):
            chain = way * 2 + sub
            rs_copy(n - 2, chain).wait_recv()
            recon = sums[n - 1, chain].astype(jnp.float32) + own_term(way, sub) + bias_ref[:, wide]
            target_rows = pl.ds(chain * sub_rows, sub_rows)
            resid[pos, target_rows, :] = (
                2.0 / total_rows * (recon - acts[target_rows, :].astype(jnp.float32))
            ).astype(jnp.bfloat16)
            ag_copy(0, 0, chain).start()
            ag_copy(1, 0, chain).start()

    def compute(shard, sub, fresh=False):
        if sub >= pieces:
            return
        lat_slice = pl.ds(sub * piece, piece)
        block = resid[shard]
        term = lax.dot_general(
            block,
            dec_block(shard, lat_slice),
            (((1,), (1,)), ((), ())),
            preferred_element_type=jnp.float32,
        )
        if fresh:
            code_grad[:, lat_slice] = term
        else:
            code_grad[:, lat_slice] += term
        grad = jnp.dot(
            codes_t[lat_slice, :], block, preferred_element_type=jnp.float32
        ).astype(jnp.bfloat16)
        outgoing[shard, lat_slice, :] = grad
        if sub == pieces - 1:
            @pl.when(lax.rem(shard, 2) != row)
            def _():
                exchange(shard // 2).start()

    def forward(step, sub):
        for way in range(2):
            ag_copy(way, step, sub).wait_recv()
            if sub // 2 == way:
                ag_copy(way, step + 1, sub).start()
            else:

                @pl.when(step < half - 2)
                def _():
                    ag_copy(way, step + 1, sub).start()

    for sub in range(subs):
        compute(pos, sub, fresh=True)
        forward(0, sub)

    @pl.loop(1, half - 1)
    def _(step):
        for sub in range(subs):
            compute(shard_at(-step), sub)
            compute(shard_at(step), sub)
            forward(step, sub)
            if sub == 0:
                adam_block(shard_at(1 - step))
            if sub == 2:

                @pl.when(step > 1)
                def _():
                    adam_block(shard_at(step - 1))


    for sub in range(subs):
        compute(shard_at(1 - half), sub)
        compute(shard_at(half - 1), sub)
    adam_block(shard_at(2 - half))
    adam_block(shard_at(half - 2))
    for sub in range(subs):
        ag_copy(sub // 2, half - 1, sub).wait_recv()
    for sub in range(subs):
        compute(shard_at(half), sub)
    pre_grad_ref[...] = jnp.where(
        preact[...] > 0, code_grad[...] + l1_weight / total_rows, 0.0
    ).astype(jnp.bfloat16)
    adam_block(shard_at(1 - half))
    adam_block(shard_at(half - 1))
    adam_block(shard_at(half))

    @pl.loop(0, n - 1)
    def _(step):
        for chain in range(subs):
            rs_copy(step, chain).wait_send()

    @pl.loop(0, half - 1)
    def _(step):
        for way in range(2):
            for sub in range(subs):
                ag_copy(way, step, sub).wait_send()

    for sub in range(subs):
        ag_copy(sub // 2, half - 1, sub).wait_send()

    @pl.loop(0, half)
    def _(block):
        exchange(block).wait_send()
        keep(block).wait()

    @pl.loop(0, 2 * blocks)
    def _(block):
        swap_dec(block).wait_send()

    save_centered.wait()


def residual_step(
    enc_weight, dec_weight, enc_bias, dec_bias, activations, dec_first, dec_second, total_rows
):
    n = lax.axis_size("lat")
    rows, model = activations.shape
    lats = enc_weight.shape[1]
    width = model // n
    half = n // 2
    bf16, f32 = jnp.bfloat16, jnp.float32
    vmem = pl.BlockSpec(memory_space=pltpu.VMEM)
    whole = pl.BlockSpec(memory_space=pl.ANY)
    return pl.pallas_call(
        functools.partial(ring_kernel, n, n <= 8, total_rows),
        out_shape=(
            jax.ShapeDtypeStruct((rows, lats), bf16),
            jax.ShapeDtypeStruct((lats, model // 2), bf16),
            jax.ShapeDtypeStruct((rows, model), bf16),
        ),
        in_specs=[whole, whole, vmem, vmem, whole, whole, whole],
        out_specs=(vmem, whole, whole),
        scratch_shapes=[
            pltpu.VMEM((rows, lats), f32),
            pltpu.VMEM((rows, model), bf16),
            pltpu.VMEM((2, model // 2, lats), bf16),
            pltpu.VMEM((2, model // 2 // blocks, lats), f32),
            pltpu.VMEM((2, lats // blocks // 2, model // 2), f32),
            pltpu.VMEM((2, lats, model // 2), bf16),
            pltpu.VMEM((rows, width), bf16),
            pltpu.VMEM((n, subs, rows // subs, width), bf16),
            pltpu.VMEM((n, rows, width), bf16),
            pltpu.VMEM((rows, lats), bf16),
            pltpu.VMEM((lats, rows), bf16),
            pltpu.VMEM((rows, lats), f32),
            pltpu.VMEM((2, rows // 2, width), f32),
            pltpu.VMEM((n, lats, width), bf16),
            pltpu.SemaphoreType.DMA((n - 1, subs)),
            pltpu.SemaphoreType.DMA((n - 1, subs)),
            pltpu.SemaphoreType.DMA((2, half, subs)),
            pltpu.SemaphoreType.DMA((2, half, subs)),
            pltpu.SemaphoreType.DMA((half,)),
            pltpu.SemaphoreType.DMA((half,)),
            pltpu.SemaphoreType.DMA((3,)),
            pltpu.SemaphoreType.DMA((2,)),
            pltpu.SemaphoreType.DMA((2,)),
            pltpu.SemaphoreType.DMA((blocks,)),
            pltpu.SemaphoreType.DMA((blocks,)),
            pltpu.SemaphoreType.DMA((2 * blocks,)),
            pltpu.SemaphoreType.DMA((2 * blocks,)),
            pltpu.SemaphoreType.DMA((half,)),
            pltpu.SemaphoreType.DMA((2, half)),
            pltpu.VMEM((half, lats, width), bf16),
        ],
        compiler_params=pltpu.CompilerParams(
            collective_id=0, has_side_effects=True, vmem_limit_bytes=62 * 1024 * 1024
        ),
        cost_estimate=pl.CostEstimate(
            flops=8 * rows * lats * model, bytes_accessed=30 * 1024 * 1024, transcendentals=0
        ),
    )(
        enc_weight,
        dec_weight,
        enc_bias.reshape(1, -1),
        dec_bias.reshape(1, -1),
        activations,
        dec_first,
        dec_second,
    )


def on_device(
    activations,
    enc_weight,
    dec_weight,
    enc_bias,
    dec_bias,
    enc_first,
    enc_second,
    dec_first,
    dec_second,
):
    total_rows = activations.shape[0] * lax.axis_size("row")
    row = lax.axis_index("row")
    part = enc_weight.shape[0]
    swap = [(0, 1), (1, 0)]
    pre_grad, dec_step, centered = residual_step(
        enc_weight, dec_weight, enc_bias, dec_bias, activations, dec_first, dec_second, total_rows
    )
    centered_own = lax.dynamic_slice_in_dim(centered, row * part, part, 1)
    centered_peer = lax.dynamic_slice_in_dim(centered, (1 - row) * part, part, 1)
    grad_out = rows_product(centered_peer, pre_grad).astype(jnp.bfloat16)
    grad_in = lax.ppermute(grad_out, "row", swap)
    grad_own = lax.optimization_barrier(rows_product(centered_own, pre_grad))
    grad_enc = grad_own + grad_in.astype(jnp.float32)
    return (adam_step(grad_enc, enc_first, enc_second), dec_step)


def solution(mesh):
    return jax.shard_map(
        on_device,
        mesh=mesh,
        in_specs=(
            P(("grp", "row"), None),
            P(("grp", "row"), "lat"),
            P(("grp", "lat"), "row"),
            P(("grp", "lat")),
            P("grp"),
            P(("grp", "row"), "lat"),
            P(("grp", "row"), "lat"),
            P(("grp", "lat"), "row"),
            P(("grp", "lat"), "row"),
        ),
        out_specs=(P(("grp", "row"), "lat"), P(("grp", "lat"), "row")),
        check_vma=False,
    )
```
